32 devices in a mesh: row: 16 (over z, y, core), col: 2 (over x).
Axes of the slice: x: 2, y: 2, z: 4, core: 2. Of those that a mesh axis runs over, the one named last changes fastest.
Arguments:
- grad: bfloat16 [3072, 3072], P('row', 'col'), may hold values from -0.75 to 0.75
- left_basis: bfloat16 [3072, 3072], P('row', 'col'), may hold values from -0.109375 to 0.109375
- right_basis: bfloat16 [3072, 3072], P('col', 'row'), may hold values from -0.109375 to 0.109375
- first_moment: float32 [3072, 3072], P('col', 'row'), may hold values from -0.625 to 0.625
- second_moment: float32 [3072, 3072], P('col', 'row'), may hold values from 0.002 to 0.05
- left_factor: float32 [3072, 3072], P('col', 'row'), may hold values from -6 to 6
- right_factor: float32 [3072, 3072], P('col', 'row'), may hold values from -6 to 6
Outputs:
- update: float32 [3072, 3072], P('row', 'col')
- new_first: float32 [3072, 3072], P('col', 'row')
- new_second: float32 [3072, 3072], P('col', 'row')
- new_left: float32 [3072, 3072], P('col', 'row')
- new_right: float32 [3072, 3072], P('col', 'row')
The draws below stay inside these ranges and needn't reach their ends.
All inputs are finite; a program needn't handle non-finite values.
Results may differ from the reference program's by a relative error of at most 0.005.
Values may be sent and summed in bfloat16 or wider, within the bound.
No kernel may reach another device: no remote copies, remote signals or barrier semaphores. Data moves between devices by JAX's collectives and lax.ppermute only.
A program may use at most 128 MiB of HBM per device.

```python
import math
import jax
import jax.numpy as jnp
from jax import lax

M = 3072
N = 3072


def levels(own_key, dims, shards, smallest, high):
    def one(position, shards_of):
        heights = jax.random.uniform(jax.random.fold_in(jax.random.fold_in(own_key, 6), position), (shards_of,), jnp.float32, smallest / len(shards), high / len(shards))
        return jnp.repeat(jnp.exp(heights), dims[position] // shards_of).reshape((-1,) + (1,) * (len(dims) - position - 1))

    gain = one(*shards[0])
    for cut in shards[1:]:
        gain = gain * one(*cut)
    return gain


def normal_values(own_key, dims, scale, bound, split=(), held_as=jnp.bfloat16):
    result = scale * jax.random.normal(own_key, dims, jnp.float32)
    if split:
        result = result * levels(own_key, dims, split, -0.22, 0.18)
    return jnp.clip(result, -bound, bound).astype(held_as)


def setup_inputs(seed: int = 0) -> dict:
    seeds = jax.random.split(jax.random.key(seed), 8)
    grad = normal_values(seeds[0], (M, N), 0.125, 0.75, ((0, 16), (1, 2)))
    left_basis = normal_values(seeds[1], (M, M), M ** -0.5, 0.109375, ((0, 16), (1, 2)))
    right_basis = normal_values(seeds[2], (N, N), N ** -0.5, 0.109375, ((0, 2), (1, 16)))
    first_moment = normal_values(seeds[3], (N, M), 0.1, 0.625, ((0, 2), (1, 16)), jnp.float32)
    second_moment = jnp.clip(jnp.exp(math.log(0.05) - 3.218876 * jax.random.uniform(seeds[4], (N, M), jnp.float32) ** levels(seeds[4], (N, M), ((0, 2), (1, 16)), -0.2, 0.2)), 0.002, 0.05)
    left_factor = normal_values(seeds[5], (M, M), 1.0, 6.0, ((0, 2), (1, 16)), jnp.float32)
    right_factor = normal_values(seeds[6], (N, N), 1.0, 6.0, ((0, 2), (1, 16)), jnp.float32)
    return {"grad": grad, "left_basis": left_basis, "right_basis": right_basis, "first_moment": first_moment, "second_moment": second_moment, "left_factor": left_factor, "right_factor": right_factor}


def reference(grad, left_basis, right_basis, first_moment, second_moment, left_factor, right_factor):
    left_proj = jnp.dot(left_basis.T, grad, preferred_element_type=jnp.float32).astype(jnp.bfloat16)
    rotated = jnp.dot(right_basis.T, left_proj.T, preferred_element_type=jnp.float32)
    new_first = 0.9 * first_moment + 0.1 * rotated
    new_second = 0.95 * second_moment + 0.05 * rotated * rotated
    bias_one = 1.0 - 0.9 ** 10
    bias_two = 1.0 - 0.95 ** 10
    direction = (new_first / bias_one / (jnp.sqrt(new_second / bias_two) + 1e-08)).astype(jnp.bfloat16)
    half_back = jnp.dot(direction.T, right_basis.T, preferred_element_type=jnp.float32)
    update = jnp.dot(left_basis.astype(jnp.float32), half_back, precision=lax.Precision.HIGHEST)
    left_sum = jnp.dot(grad, grad.T, preferred_element_type=jnp.float32)
    right_sum = jnp.dot(grad.T, grad, preferred_element_type=jnp.float32)
    new_left = 0.95 * left_factor + 0.05 * left_sum
    new_right = 0.95 * right_factor + 0.05 * right_sum
    return (update, new_first, new_second, new_left, new_right)
```

```python
import jax
import jax.numpy as jnp
from jax import lax
from jax.sharding import PartitionSpec as P

BF16 = jnp.bfloat16
F32 = jnp.float32


def dot(left, right, left_dim, right_dim):
    return lax.dot_general(
        left, right, (((left_dim,), (right_dim,)), ((), ())), preferred_element_type=F32
    )


def after(value, *earlier):
    return lax.optimization_barrier((value, *earlier))[0]


def solution(mesh):
    rows, X = mesh.shape["row"], mesh.shape["col"]
    A = rows // 4

    def sender(to):
        pairs = []
        for row in range(rows):
            for x in range(X):
                z, y, c, w = to(row // 4, row // 2 % 2, row % 2, x)
                pairs.append((row * X + x, ((z * 2 + y) * 2 + c) * X + w))
        return lambda value: lax.ppermute(value, ("row", "col"), pairs)

    flip_y = sender(lambda z, y, c, x: (z, 1 - y, c, x))
    flip_c = sender(lambda z, y, c, x: (z, y, 1 - c, x))
    up = sender(lambda z, y, c, x: ((z + 1) % A, y, c, x))
    along_x = [sender(lambda z, y, c, x, s=s: (z, y, c, (x + s) % X)) for s in range(X)]

    def plane_gather(mine):
        other_y = flip_y(mine)
        return [mine, flip_c(mine), other_y, flip_c(other_y)]

    def plane_scatter(blocks):
        got = flip_c(jnp.concatenate([blocks[1], blocks[3]]).astype(BF16)).astype(F32)
        height = blocks[0].shape[0]
        mine, other = blocks[0] + got[:height], blocks[2] + got[height:]
        return mine + flip_y(other.astype(BF16)).astype(F32)

    def on_device(grad, left_basis, right_basis, first, second, left_factor, right_factor):
        b, width = grad.shape
        row, x = lax.axis_index("row"), lax.axis_index("col")
        z, y, c = row // 4, row // 2 % 2, row % 2
        per = A // X
        wide = 4 * b

        def at(blocks, index):
            return lax.dynamic_index_in_dim(blocks, index, 0, keepdims=False)

        left_plane = jnp.concatenate(plane_gather(left_basis))
        grad_plane = jnp.concatenate(plane_gather(grad))
        want = (jnp.arange(per * b) // b) * wide + row % 4 * b + jnp.arange(per * b) % b
        pick = (jnp.arange(width)[:, None] == want[None, :]).astype(BF16)
        mine = dot(pick, left_plane, 0, 1).astype(BF16)
        parts = jnp.stack([mine] + [along_x[s](mine) for s in range(1, X)])
        left_cols = jnp.concatenate([at(parts, (x - w) % X) for w in range(X)]).reshape(A, b, wide)
        left_at = [at(left_cols, (z - r) % A) for r in range(A)]

        right = jnp.zeros((A, 2, 2, b, width), BF16)
        block = right_basis.T
        for r in range(A):
            for k, piece in enumerate(plane_gather(block)):
                place = ((z - r) % A, y ^ (k // 2), c ^ (k % 2), 0, 0)
                right = lax.dynamic_update_slice(right, piece[None, None, None], place)
            if r < A - 1:
                block = up(block)
        right = right.reshape(rows * b, width)

        total = dot(left_at[1], grad_plane, 1, 0)
        for r in range(2, A + 1):
            total = up(total.astype(BF16)).astype(F32) + dot(left_at[r % A], grad_plane, 1, 0)
        left_proj = total.astype(BF16)

        rotate = dot(left_proj, right, 1, 1)
        rotated = lax.dynamic_slice_in_dim(rotate, x * width, width, 1)
        for s in range(1, X):
            piece = lax.dynamic_slice_in_dim(rotate, (x + s) % X * width, width, 1)
            rotated += along_x[s](piece.astype(BF16)).astype(F32)
        new_first = 0.9 * first.T + 0.1 * rotated
        new_second = 0.95 * second.T + 0.05 * rotated * rotated
        bias_one = 1.0 - 0.9**10
        bias_two = 1.0 - 0.95**10
        direction = (new_first / bias_one / (jnp.sqrt(new_second / bias_two) + 1e-08)).astype(BF16)
        parts = jnp.stack([direction] + [along_x[s](direction) for s in range(1, X)])
        direction = jnp.concatenate([at(parts, (x - w) % X) for w in range(X)], axis=1)
        half = dot(direction, right, 1, 0).astype(BF16)

        block = after(grad, left_proj)
        grads = [block]
        for r in range(1, A):
            block = up(block)
            grads.append(block)

        update = dot(left_at[0], half, 0, 0)
        for r in range(1, A):
            half = up(half)
            update += dot(left_at[r], half, 0, 0)
        update = plane_scatter(jnp.split(update, 4))

        have = jnp.concatenate(grads)
        span = width // per
        mine = lax.dynamic_slice_in_dim(have, z % per * span, span, 1)
        cols = mine
        for s in range(1, X):
            pairs = []
            for q in range(rows):
                source = q // 4 // per
                pairs.append((q * X + source, q * X + (source + s) % X))
            got = lax.ppermute(mine, ("row", "col"), pairs)
            cols = jnp.where((z // per + s) % X == x, got, cols)
        term = dot(cols, have, 0, 0).reshape(4, span // 4, width)
        right_sum = plane_scatter([at(term, (row % 4) ^ k) for k in range(4)])
        new_right = 0.95 * right_factor.T + 0.05 * right_sum

        stacked = jnp.stack(grads)
        ordered = jnp.concatenate([at(stacked, (z - w) % A) for w in range(A)])
        term = dot(grad_plane, ordered, 1, 1)
        left_sum = lax.dynamic_slice_in_dim(term, x * per * b, per * b, 1)
        for s in range(1, X):
            piece = lax.dynamic_slice_in_dim(term, (x + s) % X * per * b, per * b, 1)
            left_sum += along_x[s](piece.astype(BF16)).astype(F32)
        own, core, over, cross = jnp.split(left_sum.astype(BF16), 4)
        got = flip_c(jnp.concatenate([core, cross]))
        over_pair = flip_y(jnp.concatenate([over, got[b:]], axis=1))
        joined = jnp.concatenate([own, got[:b], over_pair], axis=1)
        k, p, i = jnp.arange(4)[:, None, None], jnp.arange(per)[:, None], jnp.arange(b)
        goes = (p * wide + (k ^ (row % 4)) * b + i).reshape(-1)
        order = (goes[:, None] == jnp.arange(width)[None, :]).astype(BF16)
        new_left = 0.95 * left_factor.T + 0.05 * dot(joined, order, 1, 0)
        return update, new_first.T, new_second.T, new_left.T, new_right.T

    slab, turned = P("row", "col"), P("col", "row")
    return jax.shard_map(
        on_device,
        mesh=mesh,
        in_specs=(slab, slab) + (turned,) * 5,
        out_specs=(slab,) + (turned,) * 4,
        check_vma=False,
    )
```

```python
import jax
import jax.numpy as jnp
from jax import lax
from jax.sharding import PartitionSpec as P

BF16 = jnp.bfloat16
F32 = jnp.float32


def dot(left, right, left_dim, right_dim):
    return lax.dot_general(
        left, right, (((left_dim,), (right_dim,)), ((), ())), preferred_element_type=F32
    )


def tie(*values):
    return lax.optimization_barrier(values)


def solution(mesh):
    rows, X = mesh.shape["row"], mesh.shape["col"]
    A = rows // 4

    def sender(to):
        pairs = []
        for row in range(rows):
            for x in range(X):
                z, y, c, w = to(row // 4, row // 2 % 2, row % 2, x)
                pairs.append((row * X + x, ((z * 2 + y) * 2 + c) * X + w))
        return lambda value: lax.ppermute(value, ("row", "col"), pairs)

    flip_y = sender(lambda z, y, c, x: (z, 1 - y, c, x))
    flip_c = sender(lambda z, y, c, x: (z, y, 1 - c, x))
    up = sender(lambda z, y, c, x: ((z + 1) % A, y, c, x))
    along_x = [sender(lambda z, y, c, x, s=s: (z, y, c, (x + s) % X)) for s in range(X)]

    def plane_scatter(blocks):
        got = flip_c(jnp.concatenate([blocks[1], blocks[3]]).astype(BF16)).astype(F32)
        height = blocks[0].shape[0]
        mine, other = blocks[0] + got[:height], blocks[2] + got[height:]
        return mine + flip_y(other.astype(BF16)).astype(F32)

    def on_device(grad, left_basis, right_basis, first, second, left_factor, right_factor):
        b, width = grad.shape
        row, x = lax.axis_index("row"), lax.axis_index("col")
        z, y, c = row // 4, row // 2 % 2, row % 2
        per = A // X
        wide = 4 * b
        cuts = [(0, width // 2), (width // 2, width)]

        def at(blocks, index):
            return lax.dynamic_index_in_dim(blocks, index, 0, keepdims=False)

        def pick(rows_, side):
            k = jnp.arange(per * b)
            want = k // b * wide + (side * 2 + c) * b + k % b
            ones = (jnp.arange(width)[:, None] == want[None, :]).astype(BF16)
            return dot(ones, rows_, 0, 1).astype(BF16)

        rights = [right_basis.T]
        for r in range(1, A):
            rights.append(up(rights[-1]))
        left_rows = jnp.concatenate([left_basis, flip_c(left_basis)])
        left_y, grad = tie(pick(left_rows, 1 - y), grad)
        left_y, grad_y, grad_c = flip_y(left_y), flip_y(grad), flip_c(grad)
        left_mine = pick(left_rows, y)
        parts = [jnp.concatenate([left_mine, left_y], axis=1)]
        for s in range(1, X):
            parts.append(jnp.concatenate([along_x[s](left_mine), along_x[s](left_y)], axis=1))
        parts = jnp.stack(parts)
        left_cols = jnp.concatenate([at(parts, (x - w) % X) for w in range(X)]).reshape(A, b, wide)
        left_at = [at(left_cols, (z - r) % A) for r in range(A)]
        grad_yc = flip_c(grad_y)
        grad_plane = jnp.concatenate([grad, grad_c, grad_y, grad_yc])

        sums = [dot(left_at[1], grad_plane[:, lo:hi], 1, 0) for lo, hi in cuts]
        for r in range(2, A + 1):
            sums = [total.astype(BF16) for total in sums]
            if r < A:
                sums[0], rights[r] = tie(sums[0], rights[r])
            sums = [up(total) for total in sums]
            sums = [
                total.astype(F32) + dot(left_at[r % A], grad_plane[:, lo:hi], 1, 0)
                for total, (lo, hi) in zip(sums, cuts)
            ]
        left_proj = jnp.concatenate([total.astype(BF16) for total in sums], axis=1)

        right = jnp.zeros((A, 2, 2, b, width), BF16)
        for r, block in enumerate(rights):
            block, grad_y = tie(block, grad_y)
            other = flip_y(block)
            from_z = (z - r) % A
            q = (from_z // per - x) % X * per + from_z % per
            for k, piece in enumerate([block, flip_c(block), other, flip_c(other)]):
                place = (q, y ^ (k // 2), c ^ (k % 2), 0, 0)
                right = lax.dynamic_update_slice(right, piece[None, None, None], place)
        right = right.reshape(rows * b, width)

        grads, left_proj = tie(grad, left_proj)
        grads = [grads]
        for r in range(1, A):
            grads.append(up(grads[-1]))

        parts = [slice(p * wide, (p + 1) * wide) for p in range(per)]
        rotate = dot(left_proj, right, 1, 1)
        got = [[] for _ in parts]
        for s in range(1, X):
            for p in range(per):
                lo = s * width + p * wide
                got[p].append(along_x[s](rotate[:, lo : lo + wide].astype(BF16)))
        new_first, new_second, direction = [], [], []
        for p, part in enumerate(parts):
            rotated = rotate[:, part]
            for piece in got[p]:
                rotated += piece.astype(F32)
            new_first.append(0.9 * first.T[:, part] + 0.1 * rotated)
            new_second.append(0.95 * second.T[:, part] + 0.05 * rotated * rotated)
            bias_one = 1.0 - 0.9**10
            bias_two = 1.0 - 0.95**10
            root = jnp.sqrt(new_second[p] / bias_two) + 1e-08
            direction.append((new_first[p] / bias_one / root).astype(BF16))
        for s in range(X - 1, 0, -1):
            direction += [along_x[s](piece) for piece in direction[:per]]
        half = dot(jnp.concatenate(direction, axis=1), right, 1, 0).astype(BF16)
        halves = [half[:, lo:hi] for lo, hi in cuts]

        have = jnp.concatenate(grads)
        span = width // per
        cols = []
        for r, block in enumerate(grads):
            mine = lax.dynamic_slice_in_dim(block, z % per * span, span, 1)
            if r:
                mine, halves[1] = tie(mine, halves[1])
            take = mine
            for s in range(1, X):
                pairs = []
                for q in range(rows):
                    source = q // 4 // per
                    pairs.append((q * X + source, q * X + (source + s) % X))
                sent = lax.ppermute(mine, ("row", "col"), pairs)
                take = jnp.where((z // per + s) % X == x, sent, take)
            cols.append(take)
        cols = jnp.concatenate(cols)

        term = dot(cols, have, 0, 0).reshape(4, span // 4, width)
        right_sum = plane_scatter([at(term, (row % 4) ^ k) for k in range(4)])

        grad_rows = jnp.concatenate([grad, grad_c, grad_y, grad_yc])
        stacked = jnp.stack(grads)
        ordered = jnp.concatenate([at(stacked, (z - w) % A) for w in range(A)])
        term = dot(grad_rows, ordered, 1, 1)
        left_sum = lax.dynamic_slice_in_dim(term, x * per * b, per * b, 1)
        for s in range(1, X):
            piece = lax.dynamic_slice_in_dim(term, (x + s) % X * per * b, per * b, 1)
            left_sum += along_x[s](piece.astype(BF16)).astype(F32)
        own, core, over, cross = jnp.split(left_sum.astype(BF16), 4)
        got = flip_c(jnp.concatenate([core, cross]))
        over_pair = flip_y(jnp.concatenate([over, got[b:]], axis=1))
        joined = jnp.concatenate([own, got[:b], over_pair], axis=1)
        update = [dot(left_at[0], half, 0, 0) for half in halves]
        for r in range(1, A):
            halves = [up(half) for half in halves]
            if r == A - 1:
                halves[0], right_sum, joined = tie(halves[0], right_sum, joined)
            update = [total + dot(left_at[r], half, 0, 0) for total, half in zip(update, halves)]
        update = jnp.concatenate([plane_scatter(jnp.split(u, 4)) for u in update], axis=1)

        k, p, i = jnp.arange(4)[:, None, None], jnp.arange(per)[:, None], jnp.arange(b)
        goes = (p * wide + (k ^ (row % 4)) * b + i).reshape(-1)
        order = (goes[:, None] == jnp.arange(width)[None, :]).astype(BF16)
        new_right = 0.95 * right_factor.T + 0.05 * right_sum
        new_left = 0.95 * left_factor.T + 0.05 * dot(joined, order, 1, 0)
        new_first, new_second = (jnp.concatenate(v, axis=1) for v in (new_first, new_second))
        return update, new_first.T, new_second.T, new_left.T, new_right.T

    slab, turned = P("row", "col"), P("col", "row")
    return jax.shard_map(
        on_device,
        mesh=mesh,
        in_specs=(slab, slab) + (turned,) * 5,
        out_specs=(slab,) + (turned,) * 4,
        check_vma=False,
    )
```

```python
import jax
import jax.numpy as jnp
from jax import lax
from jax.sharding import PartitionSpec as P

BF16 = jnp.bfloat16
F32 = jnp.float32


def dot(left, right, left_dim, right_dim):
    return lax.dot_general(
        left, right, (((left_dim,), (right_dim,)), ((), ())), preferred_element_type=F32
    )


def tie(*values):
    return lax.optimization_barrier(values)


def solution(mesh):
    rows, X = mesh.shape["row"], mesh.shape["col"]
    A = rows // 4

    def sender(to):
        pairs = []
        for row in range(rows):
            for x in range(X):
                z, y, c, w = to(row // 4, row // 2 % 2, row % 2, x)
                pairs.append((row * X + x, ((z * 2 + y) * 2 + c) * X + w))
        return lambda value: lax.ppermute(value, ("row", "col"), pairs)

    flip_y = sender(lambda z, y, c, x: (z, 1 - y, c, x))
    flip_c = sender(lambda z, y, c, x: (z, y, 1 - c, x))
    up = sender(lambda z, y, c, x: ((z + 1) % A, y, c, x))
    along_x = [sender(lambda z, y, c, x, s=s: (z, y, c, (x + s) % X)) for s in range(X)]

    def plane_scatter(blocks):
        got = flip_c(jnp.concatenate([blocks[1], blocks[3]]).astype(BF16)).astype(F32)
        height = blocks[0].shape[0]
        mine, other = blocks[0] + got[:height], blocks[2] + got[height:]
        return mine + flip_y(other.astype(BF16)).astype(F32)

    def on_device(grad, left_basis, right_basis, first, second, left_factor, right_factor):
        b, width = grad.shape
        row, x = lax.axis_index("row"), lax.axis_index("col")
        z, y, c = row // 4, row // 2 % 2, row % 2
        per = A // X
        wide = 4 * b
        cuts = [(0, width // 2), (width // 2, width)]

        def at(blocks, index):
            return lax.dynamic_index_in_dim(blocks, index, 0, keepdims=False)

        def pick(rows_, side):
            k = jnp.arange(per * b)
            want = k // b * wide + (side * 2 + c) * b + k % b
            ones = (jnp.arange(width)[:, None] == want[None, :]).astype(BF16)
            return dot(ones, rows_, 0, 1).astype(BF16)

        rights = [right_basis.T]
        for r in range(1, A):
            rights.append(up(rights[-1]))
        left_rows = jnp.concatenate([left_basis, flip_c(left_basis)])
        left_y, grad = tie(pick(left_rows, 1 - y), grad)
        left_y, grad_y, grad_c = flip_y(left_y), flip_y(grad), flip_c(grad)
        left_mine = pick(left_rows, y)
        parts = [jnp.concatenate([left_mine, left_y], axis=1)]
        for s in range(1, X):
            parts.append(jnp.concatenate([along_x[s](left_mine), along_x[s](left_y)], axis=1))
        parts = jnp.stack(parts)
        left_cols = jnp.concatenate([at(parts, (x - w) % X) for w in range(X)]).reshape(A, b, wide)
        left_at = [at(left_cols, (z - r) % A) for r in range(A)]
        grad_yc = flip_c(grad_y)
        grad_plane = jnp.concatenate([grad, grad_c, grad_y, grad_yc])

        sums = [dot(left_at[1], grad_plane[:, lo:hi], 1, 0) for lo, hi in cuts]
        for r in range(2, A + 1):
            sums = [total.astype(BF16) for total in sums]
            if r < A:
                sums[0], rights[r] = tie(sums[0], rights[r])
            sums = [up(total) for total in sums]
            sums = [
                total.astype(F32) + dot(left_at[r % A], grad_plane[:, lo:hi], 1, 0)
                for total, (lo, hi) in zip(sums, cuts)
            ]
        left_proj = jnp.concatenate([total.astype(BF16) for total in sums], axis=1)

        right = jnp.zeros((A, 2, 2, b, width), BF16)
        for r, block in enumerate(rights):
            block, grad_y = tie(block, grad_y)
            other = flip_y(block)
            from_z = (z - r) % A
            q = (from_z // per - x) % X * per + from_z % per
            for k, piece in enumerate([block, flip_c(block), other, flip_c(other)]):
                place = (q, y ^ (k // 2), c ^ (k % 2), 0, 0)
                right = lax.dynamic_update_slice(right, piece[None, None, None], place)
        right = right.reshape(rows * b, width)

        grads, left_proj = tie(grad, left_proj)
        grads = [grads]
        for r in range(1, A):
            grads.append(up(grads[-1]))

        parts = [slice(p * wide, (p + 1) * wide) for p in range(per)]
        rotate = dot(left_proj, right, 1, 1)
        got = [[] for _ in parts]
        for s in range(1, X):
            for p in range(per):
                lo = s * width + p * wide
                got[p].append(along_x[s](rotate[:, lo : lo + wide].astype(BF16)))
        new_first, new_second, direction = [], [], []
        for p, part in enumerate(parts):
            rotated = rotate[:, part]
            for piece in got[p]:
                rotated += piece.astype(F32)
            new_first.append(0.9 * first.T[:, part] + 0.1 * rotated)
            new_second.append(0.95 * second.T[:, part] + 0.05 * rotated * rotated)
            bias_one = 1.0 - 0.9**10
            bias_two = 1.0 - 0.95**10
            root = jnp.sqrt(new_second[p] / bias_two) + 1e-08
            direction.append((new_first[p] / bias_one / root).astype(BF16))
        for s in range(X - 1, 0, -1):
            direction += [along_x[s](piece) for piece in direction[:per]]
        half = dot(jnp.concatenate(direction, axis=1), right, 1, 0).astype(BF16)
        late, half = tie(grads[A - 2], half)
        halves = [half[:, lo:hi] for lo, hi in cuts]

        have = jnp.concatenate(grads)
        span = width // per
        cols = []
        for r, block in enumerate(grads):
            mine = lax.dynamic_slice_in_dim(block, z % per * span, span, 1)
            take = mine
            for s in range(1, X):
                sent = along_x[s](mine)
                take = jnp.where((z // per + s) % X == x, sent, take)
            cols.append(take)
        cols = jnp.concatenate(cols)

        term = dot(cols, have, 0, 0).reshape(4, span // 4, width)
        right_sum = plane_scatter([at(term, (row % 4) ^ k) for k in range(4)])

        grad_rows = jnp.concatenate([grad, grad_c, grad_y, grad_yc])
        stacked = jnp.stack(grads)
        ordered = jnp.concatenate([at(stacked, (z - w) % A) for w in range(A)])
        term = dot(grad_rows, ordered, 1, 1)
        left_sum = lax.dynamic_slice_in_dim(term, x * per * b, per * b, 1)
        for s in range(1, X):
            piece = lax.dynamic_slice_in_dim(term, (x + s) % X * per * b, per * b, 1)
            left_sum += along_x[s](piece.astype(BF16)).astype(F32)
        own, core, over, cross = jnp.split(left_sum.astype(BF16), 4)
        got = flip_c(jnp.concatenate([core, cross]))
        over_pair = flip_y(jnp.concatenate([over, got[b:]], axis=1))
        joined = jnp.concatenate([own, got[:b], over_pair], axis=1)
        update = [dot(left_at[0], half, 0, 0) for half in halves]
        for r in range(1, A):
            halves = [up(half) for half in halves]
            update = [total + dot(left_at[r], half, 0, 0) for total, half in zip(update, halves)]
        update = jnp.concatenate([plane_scatter(jnp.split(u, 4)) for u in update], axis=1)

        k, p, i = jnp.arange(4)[:, None, None], jnp.arange(per)[:, None], jnp.arange(b)
        goes = (p * wide + (k ^ (row % 4)) * b + i).reshape(-1)
        order = (goes[:, None] == jnp.arange(width)[None, :]).astype(BF16)
        new_right = 0.95 * right_factor.T + 0.05 * right_sum
        new_left = 0.95 * left_factor.T + 0.05 * dot(joined, order, 1, 0)
        new_first, new_second = (jnp.concatenate(v, axis=1) for v in (new_first, new_second))
        return update, new_first.T, new_second.T, new_left.T, new_right.T

    slab, turned = P("row", "col"), P("col", "row")
    return jax.shard_map(
        on_device,
        mesh=mesh,
        in_specs=(slab, slab) + (turned,) * 5,
        out_specs=(slab,) + (turned,) * 4,
        check_vma=False,
    )
```

```python
import jax
import jax.numpy as jnp
from jax import lax
from jax.sharding import PartitionSpec as P

BF16 = jnp.bfloat16
F32 = jnp.float32


def dot(left, right, left_dim, right_dim):
    return lax.dot_general(
        left, right, (((left_dim,), (right_dim,)), ((), ())), preferred_element_type=F32
    )


def tie(*values):
    return lax.optimization_barrier(values)


def solution(mesh):
    rows, X = mesh.shape["row"], mesh.shape["col"]
    A = rows // 4

    def sender(to):
        pairs = []
        for row in range(rows):
            for x in range(X):
                z, y, c, w = to(row // 4, row // 2 % 2, row % 2, x)
                pairs.append((row * X + x, ((z * 2 + y) * 2 + c) * X + w))
        return lambda value: lax.ppermute(value, ("row", "col"), pairs)

    flip_y = sender(lambda z, y, c, x: (z, 1 - y, c, x))
    flip_c = sender(lambda z, y, c, x: (z, y, 1 - c, x))
    up = sender(lambda z, y, c, x: ((z + 1) % A, y, c, x))
    along_x = [sender(lambda z, y, c, x, s=s: (z, y, c, (x + s) % X)) for s in range(X)]

    def core_sum(blocks):
        got = flip_c(jnp.concatenate([blocks[1], blocks[3]]).astype(BF16)).astype(F32)
        height = blocks[0].shape[0]
        return blocks[0] + got[:height], (blocks[2] + got[height:]).astype(BF16)

    def plane_scatter(blocks):
        mine, other = core_sum(blocks)
        return mine + flip_y(other).astype(F32)

    def on_device(grad, left_basis, right_basis, first, second, left_factor, right_factor):
        b, width = grad.shape
        row, x = lax.axis_index("row"), lax.axis_index("col")
        z, y, c = row // 4, row // 2 % 2, row % 2
        per = A // X
        wide = 4 * b
        cuts = [(0, width // 2), (width // 2, width)]

        def at(blocks, index):
            return lax.dynamic_index_in_dim(blocks, index, 0, keepdims=False)

        def pick(rows_, side):
            k = jnp.arange(per * b)
            want = k // b * wide + (side * 2 + c) * b + k % b
            ones = (jnp.arange(width)[:, None] == want[None, :]).astype(BF16)
            return dot(ones, rows_, 0, 1).astype(BF16)

        rights = [right_basis.T]
        for r in range(1, A):
            rights.append(up(rights[-1]))
        left_rows = jnp.concatenate([left_basis, flip_c(left_basis)])
        left_y, grad = tie(pick(left_rows, 1 - y), grad)
        left_y, grad_y, grad_c = flip_y(left_y), flip_y(grad), flip_c(grad)
        left_mine = pick(left_rows, y)
        parts = [jnp.concatenate([left_mine, left_y], axis=1)]
        for s in range(1, X):
            parts.append(jnp.concatenate([along_x[s](left_mine), along_x[s](left_y)], axis=1))
        parts = jnp.stack(parts)
        left_cols = jnp.concatenate([at(parts, (x - w) % X) for w in range(X)]).reshape(A, b, wide)
        left_at = [at(left_cols, (z - r) % A) for r in range(A)]
        grad_yc = flip_c(grad_y)
        grad_plane = jnp.concatenate([grad, grad_c, grad_y, grad_yc])

        sums = [dot(left_at[1], grad_plane[:, lo:hi], 1, 0) for lo, hi in cuts]
        for r in range(2, A + 1):
            sums = [total.astype(BF16) for total in sums]
            if r < A:
                sums[0], rights[r] = tie(sums[0], rights[r])
            sums = [up(total) for total in sums]
            sums = [
                total.astype(F32) + dot(left_at[r % A], grad_plane[:, lo:hi], 1, 0)
                for total, (lo, hi) in zip(sums, cuts)
            ]
        left_proj = jnp.concatenate([total.astype(BF16) for total in sums], axis=1)

        right = jnp.zeros((A, 2, 2, b, width), BF16)
        for r, block in enumerate(rights):
            block, grad_y = tie(block, grad_y)
            other = flip_y(block)
            from_z = (z - r) % A
            q = (from_z // per - x) % X * per + from_z % per
            for k, piece in enumerate([block, flip_c(block), other, flip_c(other)]):
                place = (q, y ^ (k // 2), c ^ (k % 2), 0, 0)
                right = lax.dynamic_update_slice(right, piece[None, None, None], place)
        right = right.reshape(rows * b, width)

        grads, left_proj = tie(grad, left_proj)
        grads = [grads]
        for r in range(1, A):
            grads.append(up(grads[-1]))

        parts = [slice(p * wide, (p + 1) * wide) for p in range(per)]
        rotate = dot(left_proj, right, 1, 1)
        got = [[] for _ in parts]
        for s in range(1, X):
            for p in range(per):
                lo = s * width + p * wide
                got[p].append(along_x[s](rotate[:, lo : lo + wide].astype(BF16)))
        new_first, new_second, direction = [], [], []
        for p, part in enumerate(parts):
            rotated = rotate[:, part]
            for piece in got[p]:
                rotated += piece.astype(F32)
            new_first.append(0.9 * first.T[:, part] + 0.1 * rotated)
            new_second.append(0.95 * second.T[:, part] + 0.05 * rotated * rotated)
            bias_one = 1.0 - 0.9**10
            bias_two = 1.0 - 0.95**10
            root = jnp.sqrt(new_second[p] / bias_two) + 1e-08
            direction.append((new_first[p] / bias_one / root).astype(BF16))
        for s in range(X - 1, 0, -1):
            direction += [along_x[s](piece) for piece in direction[:per]]
        half = dot(jnp.concatenate(direction, axis=1), right, 1, 0).astype(BF16)
        halves = [half[:, lo:hi] for lo, hi in cuts]

        have = jnp.concatenate(grads)
        span = width // per
        cols = []
        for r, block in enumerate(grads):
            mine = lax.dynamic_slice_in_dim(block, z % per * span, span, 1)
            take = mine
            for s in range(1, X):
                sent = along_x[s](mine)
                take = jnp.where((z // per + s) % X == x, sent, take)
            cols.append(take)
        cols = jnp.concatenate(cols)

        term = dot(cols, have, 0, 0).reshape(4, span // 4, width)
        right_sum, right_other = core_sum([at(term, (row % 4) ^ k) for k in range(4)])

        grad_rows = jnp.concatenate([grad, grad_c, grad_y, grad_yc])
        stacked = jnp.stack(grads)
        ordered = jnp.concatenate([at(stacked, (z - w) % A) for w in range(A)])
        term = dot(grad_rows, ordered, 1, 1)
        left_sum = lax.dynamic_slice_in_dim(term, x * per * b, per * b, 1)
        for s in range(1, X):
            piece = lax.dynamic_slice_in_dim(term, (x + s) % X * per * b, per * b, 1)
            left_sum += along_x[s](piece.astype(BF16)).astype(F32)
        update = [dot(left_at[0], half, 0, 0) for half in halves]
        for r in range(1, A):
            halves = [up(half) for half in halves]
            if r == A - 2:
                halves[1], right_other = tie(halves[1], right_other)
            if r == A - 2:
                halves[1], left_sum = tie(halves[1], left_sum)
                own, core, over, cross = jnp.split(left_sum.astype(BF16), 4)
                got = flip_c(jnp.concatenate([core, cross]))
            if r == A - 1:
                over_pair = flip_y(jnp.concatenate([over, got[b:]], axis=1))
                right_sum += flip_y(right_other).astype(F32)
            update = [total + dot(left_at[r], half, 0, 0) for total, half in zip(update, halves)]
        update = jnp.concatenate([plane_scatter(jnp.split(u, 4)) for u in update], axis=1)

        joined = jnp.concatenate([own, got[:b], over_pair], axis=1)
        k, p, i = jnp.arange(4)[:, None, None], jnp.arange(per)[:, None], jnp.arange(b)
        goes = (p * wide + (k ^ (row % 4)) * b + i).reshape(-1)
        order = (goes[:, None] == jnp.arange(width)[None, :]).astype(BF16)
        new_right = 0.95 * right_factor.T + 0.05 * right_sum
        new_left = 0.95 * left_factor.T + 0.05 * dot(joined, order, 1, 0)
        new_first, new_second = (jnp.concatenate(v, axis=1) for v in (new_first, new_second))
        return update, new_first.T, new_second.T, new_left.T, new_right.T

    slab, turned = P("row", "col"), P("col", "row")
    return jax.shard_map(
        on_device,
        mesh=mesh,
        in_specs=(slab, slab) + (turned,) * 5,
        out_specs=(slab,) + (turned,) * 4,
        check_vma=False,
    )
```

```python
import jax
import jax.numpy as jnp
from jax import lax
from jax.sharding import PartitionSpec as P

BF16 = jnp.bfloat16
F32 = jnp.float32


def dot(left, right, left_dim, right_dim):
    return lax.dot_general(
        left, right, (((left_dim,), (right_dim,)), ((), ())), preferred_element_type=F32
    )


def tie(*values):
    return lax.optimization_barrier(values)


def solution(mesh):
    rows, X = mesh.shape["row"], mesh.shape["col"]
    A = rows // 4

    def sender(to):
        pairs = []
        for row in range(rows):
            for x in range(X):
                z, y, c, w = to(row // 4, row // 2 % 2, row % 2, x)
                pairs.append((row * X + x, ((z * 2 + y) * 2 + c) * X + w))
        return lambda value: lax.ppermute(value, ("row", "col"), pairs)

    flip_y = sender(lambda z, y, c, x: (z, 1 - y, c, x))
    flip_c = sender(lambda z, y, c, x: (z, y, 1 - c, x))
    up = sender(lambda z, y, c, x: ((z + 1) % A, y, c, x))
    along_x = [sender(lambda z, y, c, x, s=s: (z, y, c, (x + s) % X)) for s in range(X)]

    def core_sum(blocks):
        got = flip_c(jnp.concatenate([blocks[1], blocks[3]]).astype(BF16)).astype(F32)
        height = blocks[0].shape[0]
        return blocks[0] + got[:height], (blocks[2] + got[height:]).astype(BF16)

    def plane_scatter(blocks):
        mine, other = core_sum(blocks)
        return mine + flip_y(other).astype(F32)

    def on_device(grad, left_basis, right_basis, first, second, left_factor, right_factor):
        b, width = grad.shape
        row, x = lax.axis_index("row"), lax.axis_index("col")
        z, y, c = row // 4, row // 2 % 2, row % 2
        per = A // X
        wide = 4 * b
        cuts = [(0, width // 2), (width // 2, width)]

        def at(blocks, index):
            return lax.dynamic_index_in_dim(blocks, index, 0, keepdims=False)

        def pick(rows_, side):
            k = jnp.arange(per * b)
            want = k // b * wide + (side * 2 + c) * b + k % b
            ones = (jnp.arange(width)[:, None] == want[None, :]).astype(BF16)
            return dot(ones, rows_, 0, 1).astype(BF16)

        rights = [right_basis.T]
        for r in range(1, A):
            rights.append(up(rights[-1]))
        left_rows = jnp.concatenate([left_basis, flip_c(left_basis)])
        left_y, grad = tie(pick(left_rows, 1 - y), grad)
        left_y, grad_y, grad_c = flip_y(left_y), flip_y(grad), flip_c(grad)
        left_mine = pick(left_rows, y)
        parts = [jnp.concatenate([left_mine, left_y], axis=1)]
        for s in range(1, X):
            parts.append(jnp.concatenate([along_x[s](left_mine), along_x[s](left_y)], axis=1))
        parts = jnp.stack(parts)
        left_cols = jnp.concatenate([at(parts, (x - w) % X) for w in range(X)]).reshape(A, b, wide)
        left_at = [at(left_cols, (z - r) % A) for r in range(A)]
        grad_yc = flip_c(grad_y)
        grad_plane = jnp.concatenate([grad, grad_c, grad_y, grad_yc])

        sums = [dot(left_at[1], grad_plane[:, lo:hi], 1, 0) for lo, hi in cuts]
        for r in range(2, A + 1):
            sums = [total.astype(BF16) for total in sums]
            if r < A:
                sums[1], rights[r] = tie(sums[1], rights[r])
            sums = [up(total) for total in sums]
            sums = [
                total.astype(F32) + dot(left_at[r % A], grad_plane[:, lo:hi], 1, 0)
                for total, (lo, hi) in zip(sums, cuts)
            ]
        left_proj = jnp.concatenate([total.astype(BF16) for total in sums], axis=1)

        right = jnp.zeros((A, 2, 2, b, width), BF16)
        for r, block in enumerate(rights):
            block, grad_y = tie(block, grad_y)
            other = flip_y(block)
            from_z = (z - r) % A
            q = (from_z // per - x) % X * per + from_z % per
            for k, piece in enumerate([block, flip_c(block), other, flip_c(other)]):
                place = (q, y ^ (k // 2), c ^ (k % 2), 0, 0)
                right = lax.dynamic_update_slice(right, piece[None, None, None], place)
        right = right.reshape(rows * b, width)

        grads, left_proj = tie(grad, left_proj)
        grads = [grads]
        for r in range(1, A):
            grads.append(up(grads[-1]))

        parts = [slice(p * wide, (p + 1) * wide) for p in range(per)]
        rotate = dot(left_proj, right, 1, 1)
        got = [[] for _ in parts]
        for s in range(1, X):
            for p in range(per):
                lo = s * width + p * wide
                got[p].append(along_x[s](rotate[:, lo : lo + wide].astype(BF16)))
        new_first, new_second, direction = [], [], []
        for p, part in enumerate(parts):
            rotated = rotate[:, part]
            for piece in got[p]:
                rotated += piece.astype(F32)
            new_first.append(0.9 * first.T[:, part] + 0.1 * rotated)
            new_second.append(0.95 * second.T[:, part] + 0.05 * rotated * rotated)
            bias_one = 1.0 - 0.9**10
            bias_two = 1.0 - 0.95**10
            root = jnp.sqrt(new_second[p] / bias_two) + 1e-08
            direction.append((new_first[p] / bias_one / root).astype(BF16))
        for s in range(X - 1, 0, -1):
            direction += [along_x[s](piece) for piece in direction[:per]]
        half = dot(jnp.concatenate(direction, axis=1), right, 1, 0).astype(BF16)
        halves = [half[:, lo:hi] for lo, hi in cuts]

        have = jnp.concatenate(grads)
        span = width // per
        cols = []
        for r, block in enumerate(grads):
            mine = lax.dynamic_slice_in_dim(block, z % per * span, span, 1)
            take = mine
            for s in range(1, X):
                sent = along_x[s](mine)
                take = jnp.where((z // per + s) % X == x, sent, take)
            cols.append(take)
        cols = jnp.concatenate(cols)

        term = dot(cols, have, 0, 0).reshape(4, span // 4, width)
        right_sum, right_other = core_sum([at(term, (row % 4) ^ k) for k in range(4)])

        grad_rows = jnp.concatenate([grad, grad_c, grad_y, grad_yc])
        stacked = jnp.stack(grads)
        ordered = jnp.concatenate([at(stacked, (z - w) % A) for w in range(A)])
        term = dot(grad_rows, ordered, 1, 1)
        left_sum = lax.dynamic_slice_in_dim(term, x * per * b, per * b, 1)
        for s in range(1, X):
            piece = lax.dynamic_slice_in_dim(term, (x + s) % X * per * b, per * b, 1)
            left_sum += along_x[s](piece.astype(BF16)).astype(F32)
        update = [dot(left_at[0], half, 0, 0) for half in halves]
        for r in range(1, A):
            halves = [up(half) for half in halves]
            if r == A - 2:
                halves[1], right_other = tie(halves[1], right_other)
            if r == A - 2:
                halves[1], left_sum = tie(halves[1], left_sum)
                own, core, over, cross = jnp.split(left_sum.astype(BF16), 4)
                got = flip_c(jnp.concatenate([core, cross]))
            if r == A - 1:
                over_pair = flip_y(jnp.concatenate([over, got[b:]], axis=1))
                right_sum += flip_y(right_other).astype(F32)
            update = [total + dot(left_at[r], half, 0, 0) for total, half in zip(update, halves)]
        update = jnp.concatenate([plane_scatter(jnp.split(u, 4)) for u in update], axis=1)

        joined = jnp.concatenate([own, got[:b], over_pair], axis=1)
        k, p, i = jnp.arange(4)[:, None, None], jnp.arange(per)[:, None], jnp.arange(b)
        goes = (p * wide + (k ^ (row % 4)) * b + i).reshape(-1)
        order = (goes[:, None] == jnp.arange(width)[None, :]).astype(BF16)
        new_right = 0.95 * right_factor.T + 0.05 * right_sum
        new_left = 0.95 * left_factor.T + 0.05 * dot(joined, order, 1, 0)
        new_first, new_second = (jnp.concatenate(v, axis=1) for v in (new_first, new_second))
        return update, new_first.T, new_second.T, new_left.T, new_right.T

    slab, turned = P("row", "col"), P("col", "row")
    return jax.shard_map(
        on_device,
        mesh=mesh,
        in_specs=(slab, slab) + (turned,) * 5,
        out_specs=(slab,) + (turned,) * 4,
        check_vma=False,
    )
```

```python
import jax
import jax.numpy as jnp
from jax import lax
from jax.sharding import PartitionSpec as P

BF16 = jnp.bfloat16
F32 = jnp.float32


def dot(left, right, left_dim, right_dim):
    return lax.dot_general(
        left, right, (((left_dim,), (right_dim,)), ((), ())), preferred_element_type=F32
    )


def tie(*values):
    return lax.optimization_barrier(values)


def solution(mesh):
    rows, X = mesh.shape["row"], mesh.shape["col"]
    A = rows // 4

    def sender(to):
        pairs = []
        for row in range(rows):
            for x in range(X):
                z, y, c, w = to(row // 4, row // 2 % 2, row % 2, x)
                pairs.append((row * X + x, ((z * 2 + y) * 2 + c) * X + w))
        return lambda value: lax.ppermute(value, ("row", "col"), pairs)

    flip_y = sender(lambda z, y, c, x: (z, 1 - y, c, x))
    flip_c = sender(lambda z, y, c, x: (z, y, 1 - c, x))
    up = sender(lambda z, y, c, x: ((z + 1) % A, y, c, x))
    along_x = [sender(lambda z, y, c, x, s=s: (z, y, c, (x + s) % X)) for s in range(X)]

    def core_sum(blocks):
        got = flip_c(jnp.concatenate([blocks[1], blocks[3]]).astype(BF16)).astype(F32)
        height = blocks[0].shape[0]
        return blocks[0] + got[:height], (blocks[2] + got[height:]).astype(BF16)

    def plane_scatter(blocks):
        mine, other = core_sum(blocks)
        return mine + flip_y(other).astype(F32)

    def on_device(grad, left_basis, right_basis, first, second, left_factor, right_factor):
        b, width = grad.shape
        row, x = lax.axis_index("row"), lax.axis_index("col")
        z, y, c = row // 4, row // 2 % 2, row % 2
        per = A // X
        wide = 4 * b
        cuts = [(0, width // 2), (width // 2, width)]

        def at(blocks, index):
            return lax.dynamic_index_in_dim(blocks, index, 0, keepdims=False)

        def pick(rows_, side):
            k = jnp.arange(per * b)
            want = k // b * wide + (side * 2 + c) * b + k % b
            ones = (jnp.arange(width)[:, None] == want[None, :]).astype(BF16)
            return dot(ones, rows_, 0, 1).astype(BF16)

        rights = [right_basis.T]
        for r in range(1, A):
            rights.append(up(rights[-1]))
        left_rows = jnp.concatenate([left_basis, flip_c(left_basis)])
        left_y, grad = tie(pick(left_rows, 1 - y), grad)
        left_y, grad_y, grad_c = flip_y(left_y), flip_y(grad), flip_c(grad)
        left_mine = pick(left_rows, y)
        parts = [jnp.concatenate([left_mine, left_y], axis=1)]
        for s in range(1, X):
            parts.append(jnp.concatenate([along_x[s](left_mine), along_x[s](left_y)], axis=1))
        parts = jnp.stack(parts)
        left_cols = jnp.concatenate([at(parts, (x - w) % X) for w in range(X)]).reshape(A, b, wide)
        left_at = [at(left_cols, (z - r) % A) for r in range(A)]
        grad_yc = flip_c(grad_y)
        grad_plane = jnp.concatenate([grad, grad_c, grad_y, grad_yc])

        sums = [dot(left_at[1], grad_plane[:, lo:hi], 1, 0) for lo, hi in cuts]
        for r in range(2, A + 1):
            sums = [total.astype(BF16) for total in sums]
            if r < A:
                sums[1], rights[r] = tie(sums[1], rights[r])
            sums = [up(total) for total in sums]
            sums = [
                total.astype(F32) + dot(left_at[r % A], grad_plane[:, lo:hi], 1, 0)
                for total, (lo, hi) in zip(sums, cuts)
            ]
        left_proj = jnp.concatenate([total.astype(BF16) for total in sums], axis=1)

        right = jnp.zeros((A, 2, 2, b, width), BF16)
        for r, block in enumerate(rights):
            block, grad_y = tie(block, grad_y)
            other = flip_y(block)
            from_z = (z - r) % A
            q = (from_z // per - x) % X * per + from_z % per
            for k, piece in enumerate([block, flip_c(block), other, flip_c(other)]):
                place = (q, y ^ (k // 2), c ^ (k % 2), 0, 0)
                right = lax.dynamic_update_slice(right, piece[None, None, None], place)
        right = right.reshape(rows * b, width)

        grads, left_proj = tie(grad, left_proj)
        grads = [grads]
        for r in range(1, A):
            grads.append(up(grads[-1]))

        parts = [slice(p * wide, (p + 1) * wide) for p in range(per)]
        rotate = dot(left_proj, right, 1, 1)
        got = [[] for _ in parts]
        for s in range(1, X):
            for p in range(per):
                lo = s * width + p * wide
                got[p].append(along_x[s](rotate[:, lo : lo + wide].astype(BF16)))
        new_first, new_second, direction = [], [], []
        for p, part in enumerate(parts):
            rotated = rotate[:, part]
            for piece in got[p]:
                rotated += piece.astype(F32)
            new_first.append(0.9 * first.T[:, part] + 0.1 * rotated)
            new_second.append(0.95 * second.T[:, part] + 0.05 * rotated * rotated)
            bias_one = 1.0 - 0.9**10
            bias_two = 1.0 - 0.95**10
            root = jnp.sqrt(new_second[p] / bias_two) + 1e-08
            direction.append((new_first[p] / bias_one / root).astype(BF16))
        for s in range(X - 1, 0, -1):
            direction += [along_x[s](piece) for piece in direction[:per]]
        half = dot(jnp.concatenate(direction, axis=1), right, 1, 0).astype(BF16)
        halves = [half[:, lo:hi] for lo, hi in cuts]

        have = jnp.concatenate(grads)
        span = width // per
        cols = []
        for r, block in enumerate(grads):
            mine = lax.dynamic_slice_in_dim(block, z % per * span, span, 1)
            take = mine
            for s in range(1, X):
                sent = along_x[s](mine)
                take = jnp.where((z // per + s) % X == x, sent, take)
            cols.append(take)
        cols = jnp.concatenate(cols)

        term = dot(cols, have, 0, 0).reshape(4, span // 4, width)
        right_sum, right_other = core_sum([at(term, (row % 4) ^ k) for k in range(4)])

        grad_rows = jnp.concatenate([grad, grad_c, grad_y, grad_yc])
        stacked = jnp.stack(grads)
        ordered = jnp.concatenate([at(stacked, (z - w) % A) for w in range(A)])
        term = dot(grad_rows, ordered, 1, 1)
        left_sum = lax.dynamic_slice_in_dim(term, x * per * b, per * b, 1)
        for s in range(1, X):
            piece = lax.dynamic_slice_in_dim(term, (x + s) % X * per * b, per * b, 1)
            left_sum += along_x[s](piece.astype(BF16)).astype(F32)
        update = [dot(left_at[0], half, 0, 0) for half in halves]
        for r in range(1, A):
            halves = [up(half) for half in halves]
            if r == A - 2:
                halves[1], left_sum = tie(halves[1], left_sum)
                own, core, over, cross = jnp.split(left_sum.astype(BF16), 4)
                got = flip_c(jnp.concatenate([core, cross]))
            if r == A - 1:
                over_pair = flip_y(jnp.concatenate([over, got[b:]], axis=1))
                halves[1], right_other = tie(halves[1], right_other)
                right_sum += flip_y(right_other).astype(F32)
            update = [total + dot(left_at[r], half, 0, 0) for total, half in zip(update, halves)]
        update = jnp.concatenate([plane_scatter(jnp.split(u, 4)) for u in update], axis=1)

        joined = jnp.concatenate([own, got[:b], over_pair], axis=1)
        k, p, i = jnp.arange(4)[:, None, None], jnp.arange(per)[:, None], jnp.arange(b)
        goes = (p * wide + (k ^ (row % 4)) * b + i).reshape(-1)
        order = (goes[:, None] == jnp.arange(width)[None, :]).astype(BF16)
        new_right = 0.95 * right_factor.T + 0.05 * right_sum
        new_left = 0.95 * left_factor.T + 0.05 * dot(joined, order, 1, 0)
        new_first, new_second = (jnp.concatenate(v, axis=1) for v in (new_first, new_second))
        return update, new_first.T, new_second.T, new_left.T, new_right.T

    slab, turned = P("row", "col"), P("col", "row")
    return jax.shard_map(
        on_device,
        mesh=mesh,
        in_specs=(slab, slab) + (turned,) * 5,
        out_specs=(slab,) + (turned,) * 4,
        check_vma=False,
    )
```
